32 devices in a mesh: pipe: 4 (over x, core), role: 2 (over y), tp: 4 (over z).
Axes of the slice: x: 2, y: 2, z: 4, core: 2. Of those that a mesh axis runs over, the one named last changes fastest.
Arguments:
- student_input: bfloat16 [512, 4096], P(('role', 'tp')), may hold values from -6 to 6
- teacher_hidden: bfloat16 [4, 512, 8192], P('pipe', None, ('role', 'tp')), may hold values from -40 to 40
- channel_order: int32 [8192], replicated, may hold values from 0 to 8191, each once
- norm_gain: float32 [4, 4096], P('pipe'), may hold values from 0.5 to 1.5
- w_gate: bfloat16 [4, 4096, 8192], P('pipe', None, ('role', 'tp')), may hold values from -0.09375 to 0.09375
- w_up: bfloat16 [4, 4096, 8192], P('pipe', None, ('role', 'tp')), may hold values from -0.09375 to 0.09375
- w_down: bfloat16 [4, 8192, 4096], P('pipe', ('role', 'tp')), may hold values from -0.0625 to 0.0625
Outputs:
- grad_gate: bfloat16 [4, 4096, 8192], P('pipe', None, ('role', 'tp'))
- grad_up: bfloat16 [4, 4096, 8192], P('pipe', None, ('role', 'tp'))
- grad_down: bfloat16 [4, 8192, 4096], P('pipe', ('role', 'tp'))
- grad_gain: float32 [4, 4096], P('pipe')
The draws below stay inside these ranges and needn't reach their ends.
Inputs may be any that keep to these rules, and one draw needn't show every extreme that they name: `channel_order`: a permutation; the first 4096 entries are the channels the student keeps.
All inputs are finite; a program needn't handle non-finite values.
Results may differ from the reference program's by a relative error of at most 0.017.
Values may be sent and summed in bfloat16 or wider, within the bound.
A program may use at most 128 MiB of HBM per device.

```python
from functools import partial
import jax
import jax.numpy as jnp
from jax import lax

D = 4096
DT = 8192
FW = 8192
ROWS = 512
SECTIONS = 4
N_ROLE = 2
N_TP = 4


def draw_teacher_hidden(key, part):
    keys = jax.random.split(jax.random.fold_in(key, 7), 1)
    base = jax.random.normal(keys[0], (SECTIONS, ROWS, DT), jnp.float32)
    section_index = jnp.arange(SECTIONS).reshape(SECTIONS, 1, 1)
    step_weight = jnp.where(section_index == 0, 1.0, 0.3).astype(jnp.float32)
    values = jnp.cumsum(base * step_weight, axis=0)
    return jnp.clip(values, -40.0, 40.0).astype(jnp.bfloat16)


def block_levels(own_key, dims, cuts, least, high):
    gain, own = 1.0, jax.random.fold_in(own_key, 6)
    for dim, parts in cuts:
        draws = jnp.exp(jax.random.uniform(jax.random.fold_in(own, dim), (parts,), jnp.float32, least / len(cuts), high / len(cuts)))
        gain = gain * jnp.repeat(draws, dims[dim] // parts).reshape([-1 if axis == dim else 1 for axis in range(len(dims))])
    return gain


def gaussian(own_key, shape, spread, reach, pieces=(), dtype=jnp.bfloat16):
    values = spread * jax.random.normal(own_key, shape, jnp.float32)
    if pieces:
        values = values * block_levels(own_key, shape, pieces, -0.22, 0.18)
    return jnp.clip(values, -reach, reach).astype(dtype)


def setup_inputs(seed: int = 0) -> dict:
    seeds = jax.random.split(jax.random.key(seed), 8)
    return {
        "student_input": gaussian(seeds[0], (ROWS, D), 1.0, 6.0, ((0, 8),)),
        "teacher_hidden": draw_teacher_hidden(jax.random.fold_in(seeds[7], 71), 0),
        "channel_order": jax.random.permutation(seeds[2], DT).astype(jnp.int32),
        "norm_gain": jnp.clip(1.0 + 0.1 * jax.random.normal(seeds[3], (SECTIONS, D), jnp.float32), 0.5, 1.5),
        "w_gate": gaussian(seeds[4], (SECTIONS, D, FW), D ** -0.5, 0.09375, ((0, 4), (2, 8))),
        "w_up": gaussian(seeds[5], (SECTIONS, D, FW), D ** -0.5, 0.09375, ((0, 4), (2, 8))),
        "w_down": gaussian(seeds[6], (SECTIONS, FW, D), FW ** -0.5, 0.0625, ((0, 4), (1, 8))),
    }


epsilon = 1e-05

def one_section(operands, kept_channels):
    source, teacher, gain_row, weight_gate, weight_up, weight_down = operands
    groups = N_ROLE * N_TP
    source_f = source.astype(jnp.float32)
    inverse = lax.rsqrt(lax.optimization_barrier(jnp.mean(source_f * source_f, axis=1, keepdims=True)) + epsilon)
    normed = (source_f * inverse * gain_row).astype(jnp.bfloat16)
    gate_pre = jnp.dot(normed, weight_gate, preferred_element_type=jnp.float32)
    up_pre = jnp.dot(normed, weight_up, preferred_element_type=jnp.float32)
    gate_sig = jax.nn.sigmoid(gate_pre)
    hidden = (gate_pre * gate_sig * up_pre).astype(jnp.bfloat16)
    row_total = hidden.shape[0]
    per_group = hidden.shape[1] // groups
    hidden_groups = hidden.reshape(row_total, groups, per_group).astype(jnp.float32)
    down_groups = weight_down.reshape(groups, per_group, -1).astype(jnp.float32)
    group_terms = jnp.einsum('rgk,gkd->grd', hidden_groups, down_groups)
    group_terms = lax.optimization_barrier(group_terms.astype(jnp.bfloat16)).astype(jnp.float32)
    branch = lax.optimization_barrier(jnp.sum(group_terms, axis=0))
    output = source_f + branch
    out_inv = lax.rsqrt(lax.optimization_barrier(jnp.mean(output * output, axis=1, keepdims=True)) + epsilon)
    out_norm = output * out_inv
    teach_f = teacher.astype(jnp.float32)
    teach_inv = lax.rsqrt(lax.optimization_barrier(jnp.mean(teach_f * teach_f, axis=1, keepdims=True)) + epsilon)
    target = jnp.take(teach_f, kept_channels, axis=1) * teach_inv
    residue = out_norm - target
    out_grad = (out_inv * (residue - out_norm * lax.optimization_barrier(jnp.mean(residue * out_norm, axis=1, keepdims=True)))).astype(jnp.bfloat16)
    act_grad = jnp.dot(out_grad, weight_down.T, preferred_element_type=jnp.float32)
    gate_grad = (act_grad * up_pre * gate_sig * (1.0 + gate_pre * (1.0 - gate_sig))).astype(jnp.bfloat16)
    up_grad = (act_grad * gate_pre * gate_sig).astype(jnp.bfloat16)
    grad_down = jnp.dot(hidden.T, out_grad, preferred_element_type=jnp.float32).astype(jnp.bfloat16)
    grad_gate = jnp.dot(normed.T, gate_grad, preferred_element_type=jnp.float32).astype(jnp.bfloat16)
    grad_up = jnp.dot(normed.T, up_grad, preferred_element_type=jnp.float32).astype(jnp.bfloat16)
    gate_groups = gate_grad.reshape(row_total, groups, per_group).astype(jnp.float32)
    up_groups = up_grad.reshape(row_total, groups, per_group).astype(jnp.float32)
    wgate_groups = weight_gate.reshape(-1, groups, per_group).astype(jnp.float32)
    wup_groups = weight_up.reshape(-1, groups, per_group).astype(jnp.float32)
    normed_terms = jnp.einsum('rgk,dgk->grd', gate_groups, wgate_groups) + jnp.einsum('rgk,dgk->grd', up_groups, wup_groups)
    normed_terms = lax.optimization_barrier(normed_terms.astype(jnp.bfloat16)).astype(jnp.float32)
    normed_grad = lax.optimization_barrier(jnp.sum(normed_terms, axis=0))
    grad_gain = lax.optimization_barrier(jnp.sum(normed_grad * source_f * inverse, axis=0))
    return (grad_gate, grad_up, grad_down, grad_gain)

def reference(student_input, teacher_hidden, channel_order, norm_gain, w_gate, w_up, w_down):
    kept_channels = channel_order[:D].astype(jnp.int32)
    chosen = jnp.take(teacher_hidden[:-1], kept_channels, axis=2)
    sources = jnp.concatenate([student_input[None], chosen], axis=0)
    results = lax.map(partial(one_section, kept_channels=kept_channels), (sources, teacher_hidden, norm_gain, w_gate, w_up, w_down))
    return (results[0], results[1], results[2], results[3])
```

```python
import jax
import jax.numpy as jnp
from jax import lax
from jax.sharding import PartitionSpec as P

epsilon = 1e-05
GROUP = ("role", "tp")
bf16 = jnp.bfloat16
f32 = jnp.float32


def passed_along(block, axis, distance):
    devices = range(lax.axis_size(axis))
    route = [(i - distance, i) for i in devices if i - distance in devices]
    return lax.ppermute(block, axis, route)


def contract(left, right, left_dim, right_dim):
    return lax.dot_general(
        left, right, (((left_dim,), (right_dim,)), ((), ())), preferred_element_type=f32
    )


def ring_routes():
    n_role, n_tp = lax.axis_size("role"), lax.axis_size("tp")
    order = []
    for row in range(n_role):
        line = [row * n_tp + column for column in range(n_tp)]
        order += line if row % 2 == 0 else line[::-1]
    n = len(order)
    right = [(order[k], order[(k + 1) % n]) for k in range(n)]
    left = [(to, frm) for frm, to in right]
    return n, right, left


def ring_step(pair, right, left):
    return lax.ppermute(pair[0], GROUP, right), lax.ppermute(pair[1], GROUP, left)


def group_sum(row):
    for axis in GROUP:
        size = lax.axis_size(axis)
        if size & (size - 1):
            row = lax.psum(row, axis)
            continue
        step = 1
        while step < size:
            row = row + lax.ppermute(row, axis, [(i, i ^ step) for i in range(size)])
            step *= 2
    return row


def joined(pieces):
    return jnp.concatenate([half for pair in pieces for half in pair], axis=0)


def per_device(student_input, teacher_hidden, channel_order, norm_gain, w_gate, w_up, w_down):
    model_width = student_input.shape[1]
    weight_gate = w_gate[0]
    weight_up = w_up[0]
    weight_down = w_down[0]
    gain_row = norm_gain[0]
    n, right, left = ring_routes()
    per = 2

    teacher = lax.all_to_all(teacher_hidden[0], GROUP, split_axis=0, concat_axis=1, tiled=True)
    kept_channels = channel_order[:model_width]
    chosen = teacher.at[:, kept_channels].get(mode="promise_in_bounds")
    previous = passed_along(chosen, "pipe", 1)
    source = jnp.where(lax.axis_index("pipe") == 0, student_input, previous)
    source_f = source.astype(f32)
    inverse = lax.rsqrt(jnp.mean(source_f * source_f, axis=1, keepdims=True) + epsilon)
    own_normed = (source_f * inverse * gain_row).astype(bf16)

    half = own_normed.shape[0] // 2
    pieces = [(own_normed[:half], own_normed[half:])]
    groups, gates, ups, hiddens, partial = [], [], [], [], []
    travelling = None
    for window in range(1, n + 4):
        arriving, passing, work = (), (), ()
        if window < n:
            arriving = ring_step(pieces[-1], right, left)
        step = window - 4
        if 1 <= step < n:
            if step == 1:
                travelling = partial[1]
            passing = ring_step(travelling, right, left)
        k, second = divmod(window - per, per)
        if 0 <= k < n // per and second == 0:
            block = joined(pieces[k * per : (k + 1) * per])
            gate_pre = jnp.dot(block, weight_gate, preferred_element_type=f32)
            up_pre = jnp.dot(block, weight_up, preferred_element_type=f32)
            hidden = (gate_pre * jax.nn.sigmoid(gate_pre) * up_pre).astype(bf16)
            work = (block, gate_pre, up_pre, hidden)
        if 0 <= k < n // per and second == per - 1:
            term = jnp.dot(hiddens[k], weight_down, preferred_element_type=f32).astype(bf16)
            work = (term,)
        arriving, passing, work = lax.optimization_barrier((arriving, passing, work))
        if arriving:
            pieces.append(arriving)
        if len(work) > 1:
            for kept, value in zip((groups, gates, ups, hiddens), work):
                kept.append(value)
        if len(work) == 1:
            for i in range(per):
                at = 2 * i * half
                partial.append((work[0][at : at + half], work[0][at + half : at + 2 * half]))
        if passing:
            mine = partial[(step + 1) % n]
            travelling = tuple(x.astype(f32) + y.astype(f32) for x, y in zip(passing, mine))
            if step + 1 < n:
                travelling = tuple(x.astype(bf16) for x in travelling)
    sum_a, sum_b = travelling
    branch = jnp.concatenate([sum_a, sum_b], axis=0).astype(f32)

    teach_f = teacher.astype(f32)
    teach_inv = lax.rsqrt(jnp.mean(teach_f * teach_f, axis=1, keepdims=True) + epsilon)
    target = chosen.astype(f32) * teach_inv
    output = source_f + branch
    out_inv = lax.rsqrt(jnp.mean(output * output, axis=1, keepdims=True) + epsilon)
    out_norm = output * out_inv
    residue = out_norm - target
    out_grad = (
        out_inv * (residue - out_norm * jnp.mean(residue * out_norm, axis=1, keepdims=True))
    ).astype(bf16)

    grad_pieces = [(out_grad[:half], out_grad[half:])]
    gain_part = jnp.zeros((model_width,), f32)
    grad_groups, gate_grads, up_grads = [], [], []
    for window in range(1, n + per):
        arriving, work = (), ()
        if window < n:
            arriving = ring_step(grad_pieces[-1], right, left)
        k, second = divmod(window - per, per)
        if k >= 0 and second == 0:
            grad_block = joined(grad_pieces[k * per : (k + 1) * per])
            gate_pre, up_pre = gates[k], ups[k]
            gate_sig = jax.nn.sigmoid(gate_pre)
            act_grad = contract(grad_block, weight_down, 1, 1)
            gate_grad = (act_grad * up_pre * gate_sig * (1.0 + gate_pre * (1.0 - gate_sig))).astype(bf16)
            up_grad = (act_grad * gate_pre * gate_sig).astype(bf16)
            work = (grad_block, gate_grad, up_grad)
        if k >= 0 and second == per - 1:
            terms = contract(gate_grads[k], weight_gate, 1, 1) + contract(
                up_grads[k], weight_up, 1, 1
            )
            work = (gain_part + jnp.sum(terms * groups[k].astype(f32), axis=0),)
        if window < n:
            arriving, work = lax.optimization_barrier((arriving, work))
            grad_pieces.append(arriving)
        if len(work) > 1:
            for kept, value in zip((grad_groups, gate_grads, up_grads), work):
                kept.append(value)
        if len(work) == 1:
            gain_part = work[0]
    grad_gain = group_sum(gain_part) / gain_row

    full_normed = jnp.concatenate(groups, axis=0)
    down_local = contract(
        jnp.concatenate(hiddens, axis=0), jnp.concatenate(grad_groups, axis=0), 0, 0
    )
    gate_local = contract(full_normed, jnp.concatenate(gate_grads, axis=0), 0, 0)
    up_local = contract(full_normed, jnp.concatenate(up_grads, axis=0), 0, 0)
    return (
        gate_local.astype(bf16)[None],
        up_local.astype(bf16)[None],
        down_local.astype(bf16)[None],
        grad_gain[None],
    )


def solution(mesh):
    placed = (
        P(GROUP, None),
        P("pipe", None, GROUP),
        P(),
        P("pipe", None),
        P("pipe", None, GROUP),
        P("pipe", None, GROUP),
        P("pipe", GROUP, None),
    )
    return jax.shard_map(
        per_device,
        mesh=mesh,
        in_specs=placed,
        out_specs=(
            P("pipe", None, GROUP),
            P("pipe", None, GROUP),
            P("pipe", GROUP, None),
            P("pipe", None),
        ),
        check_vma=False,
    )
```

```python
import jax
import jax.numpy as jnp
from jax import lax
from jax.sharding import PartitionSpec as P

epsilon = 1e-05
GROUP = ("role", "tp")
bf16 = jnp.bfloat16
f32 = jnp.float32


def passed_along(block, axis, distance):
    devices = range(lax.axis_size(axis))
    route = [(i - distance, i) for i in devices if i - distance in devices]
    return lax.ppermute(block, axis, route)


def contract(left, right, left_dim, right_dim):
    return lax.dot_general(
        left, right, (((left_dim,), (right_dim,)), ((), ())), preferred_element_type=f32
    )


def ring_routes():
    n_role, n_tp = lax.axis_size("role"), lax.axis_size("tp")
    order = []
    for row in range(n_role):
        line = [row * n_tp + column for column in range(n_tp)]
        order += line if row % 2 == 0 else line[::-1]
    n = len(order)
    right = [(order[k], order[(k + 1) % n]) for k in range(n)]
    left = [(to, frm) for frm, to in right]
    return n, right, left


def ring_step(pair, right, left):
    return lax.ppermute(pair[0], GROUP, right), lax.ppermute(pair[1], GROUP, left)


def group_sum(row):
    for axis in GROUP:
        size = lax.axis_size(axis)
        if size & (size - 1):
            row = lax.psum(row, axis)
            continue
        step = 1
        while step < size:
            row = row + lax.ppermute(row, axis, [(i, i ^ step) for i in range(size)])
            step *= 2
    return row


def joined(pieces):
    return jnp.concatenate([half for pair in pieces for half in pair], axis=0)


def per_device(student_input, teacher_hidden, channel_order, norm_gain, w_gate, w_up, w_down):
    model_width = student_input.shape[1]
    weight_gate = w_gate[0]
    weight_up = w_up[0]
    weight_down = w_down[0]
    gain_row = norm_gain[0]
    n, right, left = ring_routes()
    per = 2

    teacher = lax.all_to_all(teacher_hidden[0], GROUP, split_axis=0, concat_axis=1, tiled=True)
    kept_channels = channel_order[:model_width]
    chosen = teacher.at[:, kept_channels].get(mode="promise_in_bounds")
    previous = passed_along(chosen, "pipe", 1)
    source = jnp.where(lax.axis_index("pipe") == 0, student_input, previous)
    source_f = source.astype(f32)
    inverse = lax.rsqrt(jnp.mean(source_f * source_f, axis=1, keepdims=True) + epsilon)
    own_normed = (source_f * inverse * gain_row).astype(bf16)

    half = own_normed.shape[0] // 2
    pieces = [(own_normed[:half], own_normed[half:])]
    groups, gates, ups, hiddens, partial = [], [], [], [], []
    travelling = None
    for window in range(1, n + 4):
        arriving, passing, work = (), (), ()
        if window < n:
            arriving = ring_step(pieces[-1], right, left)
        step = window - 4
        if 1 <= step < n:
            if step == 1:
                travelling = partial[1]
            passing = ring_step(travelling, right, left)
        k, second = divmod(window - per, per)
        if 0 <= k < n // per and second == 0:
            block = joined(pieces[k * per : (k + 1) * per])
            gate_pre = jnp.dot(block, weight_gate, preferred_element_type=f32)
            up_pre = jnp.dot(block, weight_up, preferred_element_type=f32)
            hidden = (gate_pre * jax.nn.sigmoid(gate_pre) * up_pre).astype(bf16)
            work = (block, gate_pre, up_pre, hidden)
        if 0 <= k < n // per and second == per - 1:
            term = jnp.dot(hiddens[k], weight_down, preferred_element_type=f32).astype(bf16)
            work = (term,)
        arriving, passing, work = lax.optimization_barrier((arriving, passing, work))
        if arriving:
            pieces.append(arriving)
        if len(work) > 1:
            for kept, value in zip((groups, gates, ups, hiddens), work):
                kept.append(value)
        if len(work) == 1:
            for i in range(per):
                at = 2 * i * half
                partial.append((work[0][at : at + half], work[0][at + half : at + 2 * half]))
        if passing:
            mine = partial[(step + 1) % n]
            travelling = tuple(x.astype(f32) + y.astype(f32) for x, y in zip(passing, mine))
            if step + 1 < n:
                travelling = tuple(x.astype(bf16) for x in travelling)
    sum_a, sum_b = travelling
    branch = jnp.concatenate([sum_a, sum_b], axis=0).astype(f32)

    teach_f = teacher.astype(f32)
    teach_inv = lax.rsqrt(jnp.mean(teach_f * teach_f, axis=1, keepdims=True) + epsilon)
    target = chosen.astype(f32) * teach_inv
    output = source_f + branch
    out_inv = lax.rsqrt(jnp.mean(output * output, axis=1, keepdims=True) + epsilon)
    out_norm = output * out_inv
    residue = out_norm - target
    out_grad = (
        out_inv * (residue - out_norm * jnp.mean(residue * out_norm, axis=1, keepdims=True))
    ).astype(bf16)

    grad_pieces = [(out_grad[:half], out_grad[half:])]
    grad_groups, gate_grads, up_grads = [], [], []
    for window in range(1, n + 1):
        arriving, work = (), ()
        if window < n:
            arriving = ring_step(grad_pieces[-1], right, left)
        k, second = divmod(window - per, per)
        if k >= 0 and second == 0:
            grad_block = joined(grad_pieces[k * per : (k + 1) * per])
            gate_pre, up_pre = gates[k], ups[k]
            gate_sig = jax.nn.sigmoid(gate_pre)
            act_grad = contract(grad_block, weight_down, 1, 1)
            gate_grad = (act_grad * up_pre * gate_sig * (1.0 + gate_pre * (1.0 - gate_sig))).astype(bf16)
            up_grad = (act_grad * gate_pre * gate_sig).astype(bf16)
            work = (grad_block, gate_grad, up_grad)
        if window < n:
            arriving, work = lax.optimization_barrier((arriving, work))
            grad_pieces.append(arriving)
        for kept, value in zip((grad_groups, gate_grads, up_grads), work):
            kept.append(value)

    full_normed = jnp.concatenate(groups, axis=0)
    full_hidden = jnp.concatenate(hiddens, axis=0)
    full_grad = jnp.concatenate(grad_groups, axis=0)
    gate_local = contract(full_normed, jnp.concatenate(gate_grads, axis=0), 0, 0).astype(bf16)
    up_local = contract(full_normed, jnp.concatenate(up_grads, axis=0), 0, 0).astype(bf16)
    gate_local, up_local = lax.optimization_barrier((gate_local, up_local))
    gain_part = jnp.sum(gate_local.astype(f32) * weight_gate.astype(f32), axis=1) + jnp.sum(
        up_local.astype(f32) * weight_up.astype(f32), axis=1
    )
    grad_gain = group_sum(gain_part) / gain_row
    down_local = contract(full_hidden, full_grad, 0, 0)
    return (
        gate_local[None],
        up_local[None],
        down_local.astype(bf16)[None],
        grad_gain[None],
    )


def solution(mesh):
    placed = (
        P(GROUP, None),
        P("pipe", None, GROUP),
        P(),
        P("pipe", None),
        P("pipe", None, GROUP),
        P("pipe", None, GROUP),
        P("pipe", GROUP, None),
    )
    return jax.shard_map(
        per_device,
        mesh=mesh,
        in_specs=placed,
        out_specs=(
            P("pipe", None, GROUP),
            P("pipe", None, GROUP),
            P("pipe", GROUP, None),
            P("pipe", None),
        ),
        check_vma=False,
    )
```
